32 devices in a mesh: slab: 2 (over x), gal: 4 (over y, core), qb: 4 (over z).
Axes of the slice: x: 2, y: 2, z: 4, core: 2. Of those that a mesh axis runs over, the one named last changes fastest.
Arguments:
- gallery: bfloat16 [16384, 768], P(('slab', 'gal')), parts along dimension 0, may hold values from -512 to 512
- querybank: bfloat16 [8, 2048, 768], P(('slab', 'qb'), 'gal'), parts along dimension 0, may hold values from -512 to 512
- test_queries: bfloat16 [8, 512, 768], P(('slab', 'qb'), 'gal'), parts along dimension 0, may hold values from -512 to 512
Outputs:
- logprob: float32 [4096, 8192], P(('slab', 'qb'), 'gal'), parts along dimension 0
- normalizer: float32 [16384], P(('slab', 'gal')), parts along dimension 0
The draws below stay inside these ranges and needn't reach their ends.
There are 2 independent parts, one for each index of `slab`. The reference program is written for one: setup_inputs(seed, part) draws one part's arguments, and reference() takes and returns one part's arrays. A program takes and returns all parts, laid end to end along the dimension named above; each array names one. Nothing has to cross between parts.
All inputs are finite; a program needn't handle non-finite values.
Results may differ from the reference program's by a relative error of at most 0.00049.
Values may be sent and summed in bfloat16 or wider, within the bound.
A program may use at most 64 MiB of HBM per device.

```python
import math
import jax
import jax.numpy as jnp
from jax import lax

D = 768
QB_DEV = 2048
GAL_DEV = 2048
TEST_DEV = 512
CLUSTERS = 256
QB_GROUPS = 4
QBANK = 8192
GALLERY = 8192
TEST = 2048


def shared_parts(key):
    base = jax.random.fold_in(key, 11)
    centers = jnp.clip(jax.random.normal(jax.random.fold_in(base, 1), (CLUSTERS, D), jnp.float32), -4.0, 4.0)
    feature = jnp.exp(jax.random.uniform(jax.random.fold_in(base, 2), (D,), jnp.float32, 0.0, math.log(10.0)))
    return (centers, feature)


def embed_rows(key, rows, salt):
    centers, feature = shared_parts(key)
    own = jax.random.fold_in(key, salt)
    cluster = jax.random.randint(jax.random.fold_in(own, 1), (rows,), 0, CLUSTERS)
    noise = jnp.clip(jax.random.normal(jax.random.fold_in(own, 2), (rows, D), jnp.float32), -4.0, 4.0)
    center_weight, noise_weight = (0.74, 0.67)
    mixed = center_weight * centers[cluster] + noise_weight * noise
    scale = jnp.exp(jax.random.uniform(jax.random.fold_in(own, 3), (rows, 1), jnp.float32, 0.0, math.log(10.0)))
    return jnp.clip(scale * feature[None, :] * mixed, -512.0, 512.0)


def draw_gallery(key, part):
    return embed_rows(key, GALLERY, 21).astype(jnp.bfloat16)


def draw_querybank(key, part):
    return embed_rows(key, QB_GROUPS * QB_DEV, 22).reshape(QB_GROUPS, QB_DEV, D).astype(jnp.bfloat16)


def draw_test_queries(key, part):
    return embed_rows(key, QB_GROUPS * TEST_DEV, 23).reshape(QB_GROUPS, TEST_DEV, D).astype(jnp.bfloat16)


def setup_inputs(seed: int = 0, part: int = 0) -> dict:
    key_of = jax.random.split(jax.random.key(seed), 4)
    part_splits = jax.random.split(jax.random.fold_in(key_of[3], part), 4)
    return {
        "gallery": draw_gallery(jax.random.fold_in(jax.random.fold_in(key_of[3], part), 71), part),
        "querybank": draw_querybank(jax.random.fold_in(jax.random.fold_in(key_of[3], part), 71), part),
        "test_queries": draw_test_queries(jax.random.fold_in(jax.random.fold_in(key_of[3], part), 71), part),
    }


sharpness = 20.0

def unit_rows(values):
    wide = values.astype(jnp.float32)
    scaled = wide * lax.rsqrt(lax.optimization_barrier(jnp.sum(wide * wide, axis=-1, keepdims=True)) + 1e-06)
    return scaled.astype(jnp.bfloat16)

def reference(gallery, querybank, test_queries):
    gallery_unit = unit_rows(gallery)
    bank_unit = unit_rows(querybank.reshape(QBANK, D))
    test_unit = unit_rows(test_queries.reshape(TEST, D))
    blocks = gallery_unit.reshape(GALLERY // GAL_DEV, GAL_DEV, D)

    def column_block(block):
        scores = jnp.dot(bank_unit, block.T, preferred_element_type=jnp.float32)
        return lax.optimization_barrier(jnp.sum(jnp.exp(sharpness * (scores - 1.0)), axis=0))
    column_total = lax.map(column_block, blocks).reshape(GALLERY)
    normalizer = sharpness + jnp.log(column_total)
    offset = 2.0 * sharpness - math.log(QBANK)
    scores = jnp.dot(test_unit, gallery_unit.T, preferred_element_type=jnp.float32)
    logits = sharpness * scores - normalizer[None, :] - offset
    row_total = lax.optimization_barrier(jnp.sum(jnp.exp(logits), axis=1, keepdims=True))
    logprob = logits - jnp.log(row_total)
    return (logprob, normalizer)
```

```python
import functools
import math

import jax
import jax.numpy as jnp
from jax import lax
from jax.experimental import pallas as pl
from jax.experimental.pallas import tpu as pltpu
from jax.sharding import PartitionSpec as P

sharpness = 20.0
LOG2E = math.log2(math.e)
MESH = pl.DeviceIdType.MESH
WINDOW = 2


def unit(values):
    wide = values.astype(jnp.float32)
    total = jnp.sum(wide * wide, axis=-1, keepdims=True)
    return (wide * lax.rsqrt(total + 1e-06)).astype(jnp.bfloat16)


def score(rows, gallery):
    return lax.dot_general(
        rows, gallery, (((1,), (1,)), ((), ())), preferred_element_type=jnp.float32
    )


def kernel(
    gsize, qsize, gallery_hbm, bank_hbm, test_hbm,
    s_out, norm_out, row_out,
    gal, bank, test, s_buf, acc, weight, lanes, zbuf, rbuf,
    load_sem, store_sem, by_send, by_recv, bs_send, bs_recv,
    ty_send, ty_recv, ts_send, ts_recv, z_send, z_recv, r_send, r_recv,
):
    g = lax.axis_index("gal")
    q = lax.axis_index("qb")
    chips = gsize // 2
    y, core = g // 2, lax.rem(g, 2)
    sib = 2 * y + (1 - core)
    _, nb, _, cb, width = bank.shape
    _, nt, _, ct, _ = test.shape
    cols = gal.shape[0]
    bank_count = nb * cb * gsize * qsize

    loads = []
    for k in range(nb):
        loads.append(pltpu.make_async_copy(
            bank_hbm.at[pl.ds(k * cb, cb)], bank.at[y, k, core], load_sem.at[k]))
    for k in range(nt):
        loads.append(pltpu.make_async_copy(
            test_hbm.at[pl.ds(k * ct, ct)], test.at[y, k, core], load_sem.at[nb + k]))
    loads.append(pltpu.make_async_copy(gallery_hbm, gal, load_sem.at[nb + nt]))
    for copy in loads:
        copy.start()

    barrier = pltpu.get_barrier_semaphore()
    for d in range(1, gsize):
        pl.semaphore_signal(barrier, inc=1, device_id={"gal": lax.rem(g + d, gsize)}, device_id_type=MESH)
    for d in range(1, qsize):
        pl.semaphore_signal(barrier, inc=1, device_id={"qb": lax.rem(q + d, qsize)}, device_id_type=MESH)

    def across(array, sends, recvs, k, d):
        slot = array.at[y, k, core]
        there = lax.rem(y + d, chips)
        return pltpu.make_async_remote_copy(
            src_ref=slot, dst_ref=slot, send_sem=sends.at[k, d], recv_sem=recvs.at[k, d],
            device_id={"gal": 2 * there + core}, device_id_type=MESH)

    def arrival(array, sends, recvs, k, d):
        slot = array.at[lax.rem(y + chips - d, chips), k, core]
        return pltpu.make_async_remote_copy(
            src_ref=slot, dst_ref=slot, send_sem=sends.at[k, d], recv_sem=recvs.at[k, d],
            device_id={"gal": sib}, device_id_type=MESH)

    def beside(array, sends, recvs, k, d):
        slot = array.at[lax.rem(y + chips - d, chips), k, core]
        return pltpu.make_async_remote_copy(
            src_ref=slot, dst_ref=slot, send_sem=sends.at[k, d], recv_sem=recvs.at[k, d],
            device_id={"gal": sib}, device_id_type=MESH)

    def from_sib(array, sends, recvs, k, d):
        slot = array.at[lax.rem(y + chips - d, chips), k, 1 - core]
        return pltpu.make_async_remote_copy(
            src_ref=slot, dst_ref=slot, send_sem=sends.at[k, d], recv_sem=recvs.at[k, d],
            device_id={"gal": sib}, device_id_type=MESH)

    B = (bank, by_send, by_recv)
    BS = (bank, bs_send, bs_recv)
    T = (test, ty_send, ty_recv)
    TS = (test, ts_send, ts_recv)
    queue = [(B, BS, k) for k in range(nb)] + [(T, TS, k) for k in range(nt)]

    def push(i):
        if i < len(queue):
            far, near, k = queue[i]
            for d in range(1, chips):
                across(*far, k, d).start()

    for i, (far, near, k) in enumerate(queue):
        loads[i].wait()
        array = far[0]
        array[y, k, core] = unit(array[y, k, core])
        if i == 0:
            pl.semaphore_wait(barrier, gsize - 1 + qsize - 1)
        if i < WINDOW:
            push(i)
        beside(*near, k, 0).start()

    acc[...] = jnp.zeros_like(acc)
    loads[-1].wait()
    step_rows = math.gcd(cols, 64)

    @pl.loop(0, cols // step_rows)
    def _(i):
        at = pl.ds(pl.multiple_of(i * step_rows, step_rows), step_rows)
        gal[at, :] = unit(gal[at, :])

    block = math.gcd(cols, 512)

    def add_bank(slot, k):
        rows = bank[slot, k].reshape(2 * cb, width)
        for j in range(cols // block):
            at = slice(j * block, (j + 1) * block)
            part = score(rows, gal[at, :])
            part = jnp.exp2(part * (sharpness * LOG2E) - sharpness * LOG2E)
            acc[:, at] += jnp.sum(part.reshape(2 * cb // 8, 8, block), axis=0)

    stores = []

    def put_scores(slot, k):
        rows = test[slot, k].reshape(2 * ct, width)
        index = slot * nt + k
        for j in range(cols // block):
            at = slice(j * block, (j + 1) * block)
            part = score(rows, gal[at, :]) * sharpness
            s_buf[slot, 0, k, :, at] = part[:ct]
            s_buf[slot, 1, k, :, at] = part[ct:]
        for c in range(2):
            copy = pltpu.make_async_copy(
                s_buf.at[slot, c, k], s_out.at[slot, c, k], store_sem.at[slot, c, k])
            copy.start()
            stores.append(copy)

    def row_pass(slot, k):
        for c in range(2):
            total = jnp.zeros((ct, 128), jnp.float32)
            for j in range(cols // 128):
                at = slice(j * 128, (j + 1) * 128)
                part = s_buf[slot, c, k, :, at]
                total += jnp.exp2(part * LOG2E - sharpness * LOG2E) * weight[0:1, at]
            at = pl.multiple_of(((slot * 2 + c) * nt + k) * ct, ct)
            lanes[pl.ds(at, ct), :] = total

    for k in range(nb):
        from_sib(*BS, k, 0).wait_recv()
        add_bank(y, k)

    pending = None
    for i, (far, near, k) in enumerate(queue[:nb]):
        for d in range(1, chips):
            arrival(*far, k, d).wait_recv()
            beside(*near, k, d).start()
            across(*far, k, d).wait_send()
        push(i + WINDOW)
        if pending is not None:
            for d in range(1, chips):
                from_sib(*BS, pending, d).wait_recv()
                add_bank(lax.rem(y + chips - d, chips), pending)
        pending = k
    for d in range(1, chips):
        from_sib(*BS, pending, d).wait_recv()
        add_bank(lax.rem(y + chips - d, chips), pending)

    column = jnp.sum(acc[...], axis=0, keepdims=True)
    for j in range(cols // 128):
        zbuf[0, j:j + 1, :] = column[:, j * 128:(j + 1) * 128]

    def z_copy(d):
        return pltpu.make_async_remote_copy(
            src_ref=zbuf.at[0], dst_ref=zbuf.at[d], send_sem=z_send.at[d], recv_sem=z_recv.at[d],
            device_id={"qb": lax.rem(q + d, qsize)}, device_id_type=MESH)

    for d in range(1, qsize):
        z_copy(d).start()
    for k in range(nt):
        from_sib(*TS, k, 0).wait_recv()
        put_scores(y, k)
    for d in range(1, qsize):
        z_copy(d).wait_recv()
    total = zbuf[0]
    for d in range(1, qsize):
        total += zbuf[d]
    norm_out[...] = sharpness + jnp.log(total)
    scale = (bank_count * math.exp(-2.0 * sharpness)) / total
    for j in range(cols // 128):
        weight[0:1, j * 128:(j + 1) * 128] = scale[j:j + 1, :]
    for k in range(nt):
        row_pass(y, k)

    pending = None
    for i, (far, near, k) in enumerate(queue[nb:]):
        for d in range(1, chips):
            arrival(*far, k, d).wait_recv()
            beside(*near, k, d).start()
            across(*far, k, d).wait_send()
        push(nb + i + WINDOW)
        if pending is not None:
            for d in range(1, chips):
                slot = lax.rem(y + chips - d, chips)
                from_sib(*TS, pending, d).wait_recv()
                put_scores(slot, pending)
                row_pass(slot, pending)
        pending = k
    for d in range(1, chips):
        slot = lax.rem(y + chips - d, chips)
        from_sib(*TS, pending, d).wait_recv()
        put_scores(slot, pending)
        row_pass(slot, pending)

    rows = lanes.shape[0]
    rbuf[0] = jnp.zeros_like(rbuf[0])
    sums = jnp.sum(lanes[...].T, axis=0, keepdims=True)
    for j in range(rows // 128):
        rbuf[0, j:j + 1, :] = sums[:, j * 128:(j + 1) * 128]

    def r_copy(d):
        return pltpu.make_async_remote_copy(
            src_ref=rbuf.at[0], dst_ref=rbuf.at[d], send_sem=r_send.at[d], recv_sem=r_recv.at[d],
            device_id={"gal": lax.rem(g + d, gsize)}, device_id_type=MESH)

    for d in range(1, gsize):
        r_copy(d).start()
    for copy in stores:
        copy.wait()
    for i, (far, near, k) in enumerate(queue):
        for d in range(chips):
            beside(*near, k, d).wait_send()
    for d in range(1, qsize):
        z_copy(d).wait_send()
    for d in range(1, gsize):
        r_copy(d).wait()
    total = rbuf[0]
    for d in range(1, gsize):
        total += rbuf[d]
    row_out[...] = jnp.log(total)


def fused(gallery, bank, test, gsize, qsize):
    cols, width = gallery.shape
    rb, rt = bank.shape[0], test.shape[0]
    cb = math.gcd(rb, 128)
    ct = math.gcd(rt, 64)
    chips, nb, nt = gsize // 2, rb // cb, rt // ct
    rows = gsize * rt
    tall = -(-rows // 128 // 8) * 8
    dma = lambda *shape: pltpu.SemaphoreType.DMA(shape)
    f32 = jnp.float32
    scores, norm, row = pl.pallas_call(
        functools.partial(kernel, gsize, qsize),
        out_shape=(
            jax.ShapeDtypeStruct((chips, 2, nt, ct, cols), f32),
            jax.ShapeDtypeStruct((cols // 128, 128), f32),
            jax.ShapeDtypeStruct((tall, 128), f32),
        ),
        in_specs=[pl.BlockSpec(memory_space=pl.ANY)] * 3,
        out_specs=(
            pl.BlockSpec(memory_space=pl.ANY),
            pl.BlockSpec(memory_space=pltpu.VMEM),
            pl.BlockSpec(memory_space=pltpu.VMEM),
        ),
        scratch_shapes=[
            pltpu.VMEM((cols, width), jnp.bfloat16),
            pltpu.VMEM((chips, nb, 2, cb, width), jnp.bfloat16),
            pltpu.VMEM((chips, nt, 2, ct, width), jnp.bfloat16),
            pltpu.VMEM((chips, 2, nt, ct, cols), f32),
            pltpu.VMEM((8, cols), f32),
            pltpu.VMEM((8, cols), f32),
            pltpu.VMEM((rows, 128), f32),
            pltpu.VMEM((qsize, cols // 128, 128), f32),
            pltpu.VMEM((gsize, tall, 128), f32),
            dma(nb + nt + 1),
            dma(chips, 2, nt),
            dma(nb, chips), dma(nb, chips), dma(nb, chips), dma(nb, chips),
            dma(nt, chips), dma(nt, chips), dma(nt, chips), dma(nt, chips),
            dma(qsize), dma(qsize), dma(gsize), dma(gsize),
        ],
        compiler_params=pltpu.CompilerParams(
            collective_id=0, has_side_effects=True, vmem_limit_bytes=40 * 1024 * 1024
        ),
        cost_estimate=pl.CostEstimate(
            flops=2 * cols * width * gsize * (rb + rt),
            bytes_accessed=2 * width * (cols + rb + rt) + 4 * rows * cols,
            transcendentals=cols * gsize * (rb + rt),
        ),
    )(gallery, bank, test)
    return scores.reshape(rows, cols), norm.reshape(cols), row.reshape(-1)[:rows]


def per_device(gallery, querybank, test_queries):
    gsize, qsize = lax.axis_size("gal"), lax.axis_size("qb")
    bank_count = querybank.shape[1] * gsize * qsize
    offset = 2.0 * sharpness - math.log(bank_count)
    scores, normalizer, row_log = fused(gallery, querybank[0], test_queries[0], gsize, qsize)
    logprob = scores - (normalizer + offset)[None, :] - row_log[:, None]
    return (logprob, normalizer)


def solution(mesh):
    placed = (
        P(("slab", "gal"), None),
        P(("slab", "qb"), "gal", None),
        P(("slab", "qb"), "gal", None),
    )
    return jax.shard_map(
        per_device,
        mesh=mesh,
        in_specs=placed,
        out_specs=(P(("slab", "qb"), "gal"), P(("slab", "gal"))),
        check_vma=False,
    )
```

```python
import functools
import math

import jax
import jax.numpy as jnp
from jax import lax
from jax.experimental import pallas as pl
from jax.experimental.pallas import tpu as pltpu
from jax.sharding import PartitionSpec as P

sharpness = 20.0
LOG2E = math.log2(math.e)
MESH = pl.DeviceIdType.MESH
WINDOW = 2


def unit(values):
    wide = values.astype(jnp.float32)
    total = jnp.sum(wide * wide, axis=-1, keepdims=True)
    return (wide * lax.rsqrt(total + 1e-06)).astype(jnp.bfloat16)


def score(rows, gallery):
    return lax.dot_general(
        rows, gallery, (((1,), (1,)), ((), ())), preferred_element_type=jnp.float32
    )


def kernel(
    gsize, qsize, gallery_hbm, bank_hbm, test_hbm,
    s_buf, norm_out, row_out,
    gal, bank, test, acc, weight, lanes, zbuf, rbuf,
    load_sem, by_send, by_recv, bs_send, bs_recv,
    ty_send, ty_recv, ts_send, ts_recv, z_send, z_recv, r_send, r_recv,
):
    g = lax.axis_index("gal")
    q = lax.axis_index("qb")
    chips = gsize // 2
    y, core = g // 2, lax.rem(g, 2)
    sib = 2 * y + (1 - core)
    _, nb, _, cb, width = bank.shape
    _, nt, _, ct, _ = test.shape
    cols = gal.shape[0]
    bank_count = nb * cb * gsize * qsize

    loads = []
    for k in range(nb):
        loads.append(pltpu.make_async_copy(
            bank_hbm.at[pl.ds(k * cb, cb)], bank.at[y, k, core], load_sem.at[k]))
    for k in range(nt):
        loads.append(pltpu.make_async_copy(
            test_hbm.at[pl.ds(k * ct, ct)], test.at[y, k, core], load_sem.at[nb + k]))
    loads.append(pltpu.make_async_copy(gallery_hbm, gal, load_sem.at[nb + nt]))
    for copy in loads:
        copy.start()

    barrier = pltpu.get_barrier_semaphore()
    for d in range(1, gsize):
        pl.semaphore_signal(barrier, inc=1, device_id={"gal": lax.rem(g + d, gsize)}, device_id_type=MESH)
    for d in range(1, qsize):
        pl.semaphore_signal(barrier, inc=1, device_id={"qb": lax.rem(q + d, qsize)}, device_id_type=MESH)

    def across(array, sends, recvs, k, d):
        slot = array.at[y, k, core]
        there = lax.rem(y + d, chips)
        return pltpu.make_async_remote_copy(
            src_ref=slot, dst_ref=slot, send_sem=sends.at[k, d], recv_sem=recvs.at[k, d],
            device_id={"gal": 2 * there + core}, device_id_type=MESH)

    def arrival(array, sends, recvs, k, d):
        slot = array.at[lax.rem(y + chips - d, chips), k, core]
        return pltpu.make_async_remote_copy(
            src_ref=slot, dst_ref=slot, send_sem=sends.at[k, d], recv_sem=recvs.at[k, d],
            device_id={"gal": sib}, device_id_type=MESH)

    def beside(array, sends, recvs, k, d):
        slot = array.at[lax.rem(y + chips - d, chips), k, core]
        return pltpu.make_async_remote_copy(
            src_ref=slot, dst_ref=slot, send_sem=sends.at[k, d], recv_sem=recvs.at[k, d],
            device_id={"gal": sib}, device_id_type=MESH)

    def from_sib(array, sends, recvs, k, d):
        slot = array.at[lax.rem(y + chips - d, chips), k, 1 - core]
        return pltpu.make_async_remote_copy(
            src_ref=slot, dst_ref=slot, send_sem=sends.at[k, d], recv_sem=recvs.at[k, d],
            device_id={"gal": sib}, device_id_type=MESH)

    B = (bank, by_send, by_recv)
    BS = (bank, bs_send, bs_recv)
    T = (test, ty_send, ty_recv)
    TS = (test, ts_send, ts_recv)
    queue = [(B, BS, k) for k in range(nb)] + [(T, TS, k) for k in range(nt)]

    def push(i):
        if i < len(queue):
            far, near, k = queue[i]
            for d in range(1, chips):
                across(*far, k, d).start()

    for i, (far, near, k) in enumerate(queue):
        loads[i].wait()
        array = far[0]
        array[y, k, core] = unit(array[y, k, core])
        if i == 0:
            pl.semaphore_wait(barrier, gsize - 1 + qsize - 1)
        if i < WINDOW:
            push(i)
        beside(*near, k, 0).start()

    acc[...] = jnp.zeros_like(acc)
    loads[-1].wait()
    step_rows = math.gcd(cols, 64)

    @pl.loop(0, cols // step_rows)
    def _(i):
        at = pl.ds(pl.multiple_of(i * step_rows, step_rows), step_rows)
        gal[at, :] = unit(gal[at, :])

    block = math.gcd(cols, 512)

    def add_bank(slot, k):
        rows = bank[slot, k].reshape(2 * cb, width)
        for j in range(cols // block):
            at = slice(j * block, (j + 1) * block)
            part = score(rows, gal[at, :])
            part = jnp.exp2(part * (sharpness * LOG2E) - sharpness * LOG2E)
            acc[:, at] += jnp.sum(part.reshape(2 * cb // 8, 8, block), axis=0)

    def put_scores(slot, k):
        rows = test[slot, k].reshape(2 * ct, width)
        for j in range(cols // block):
            at = slice(j * block, (j + 1) * block)
            part = score(rows, gal[at, :]) * sharpness
            s_buf[slot, 0, k, :, at] = part[:ct]
            s_buf[slot, 1, k, :, at] = part[ct:]

    def row_pass(slot, k):
        for c in range(2):
            total = jnp.zeros((ct, 128), jnp.float32)
            for j in range(cols // 128):
                at = slice(j * 128, (j + 1) * 128)
                part = s_buf[slot, c, k, :, at]
                total += jnp.exp2(part * LOG2E - sharpness * LOG2E) * weight[0:1, at]
            at = pl.multiple_of(((slot * 2 + c) * nt + k) * ct, ct)
            lanes[pl.ds(at, ct), :] = total

    for k in range(nb):
        from_sib(*BS, k, 0).wait_recv()
        add_bank(y, k)
    for k in range(nt):
        from_sib(*TS, k, 0).wait_recv()
        put_scores(y, k)

    pending = None
    for i, (far, near, k) in enumerate(queue[:nb]):
        for d in range(1, chips):
            arrival(*far, k, d).wait_recv()
            beside(*near, k, d).start()
            across(*far, k, d).wait_send()
        push(i + WINDOW)
        if pending is not None:
            for d in range(1, chips):
                from_sib(*BS, pending, d).wait_recv()
                add_bank(lax.rem(y + chips - d, chips), pending)
        pending = k
    for d in range(1, chips):
        from_sib(*BS, pending, d).wait_recv()
        add_bank(lax.rem(y + chips - d, chips), pending)

    column = jnp.sum(acc[...], axis=0, keepdims=True)
    for j in range(cols // 128):
        zbuf[0, j:j + 1, :] = column[:, j * 128:(j + 1) * 128]

    def z_copy(d):
        return pltpu.make_async_remote_copy(
            src_ref=zbuf.at[0], dst_ref=zbuf.at[d], send_sem=z_send.at[d], recv_sem=z_recv.at[d],
            device_id={"qb": lax.rem(q + d, qsize)}, device_id_type=MESH)

    for d in range(1, qsize):
        z_copy(d).start()
    for d in range(1, qsize):
        z_copy(d).wait_recv()
    total = zbuf[0]
    for d in range(1, qsize):
        total += zbuf[d]
    norm_out[...] = sharpness + jnp.log(total)
    scale = (bank_count * math.exp(-2.0 * sharpness)) / total
    for j in range(cols // 128):
        weight[0:1, j * 128:(j + 1) * 128] = scale[j:j + 1, :]
    for k in range(nt):
        row_pass(y, k)

    pending = None
    for i, (far, near, k) in enumerate(queue[nb:]):
        for d in range(1, chips):
            arrival(*far, k, d).wait_recv()
            beside(*near, k, d).start()
            across(*far, k, d).wait_send()
        push(nb + i + WINDOW)
        if pending is not None:
            for d in range(1, chips):
                slot = lax.rem(y + chips - d, chips)
                from_sib(*TS, pending, d).wait_recv()
                put_scores(slot, pending)
                row_pass(slot, pending)
        pending = k
    for d in range(1, chips):
        slot = lax.rem(y + chips - d, chips)
        from_sib(*TS, pending, d).wait_recv()
        put_scores(slot, pending)
        row_pass(slot, pending)

    rows = lanes.shape[0]
    rbuf[0] = jnp.zeros_like(rbuf[0])
    sums = jnp.sum(lanes[...].T, axis=0, keepdims=True)
    for j in range(rows // 128):
        rbuf[0, j:j + 1, :] = sums[:, j * 128:(j + 1) * 128]

    def r_copy(d):
        return pltpu.make_async_remote_copy(
            src_ref=rbuf.at[0], dst_ref=rbuf.at[d], send_sem=r_send.at[d], recv_sem=r_recv.at[d],
            device_id={"gal": lax.rem(g + d, gsize)}, device_id_type=MESH)

    for d in range(1, gsize):
        r_copy(d).start()
    for i, (far, near, k) in enumerate(queue):
        for d in range(chips):
            beside(*near, k, d).wait_send()
    for d in range(1, qsize):
        z_copy(d).wait_send()
    for d in range(1, gsize):
        r_copy(d).wait()
    total = rbuf[0]
    for d in range(1, gsize):
        total += rbuf[d]
    row_out[...] = jnp.log(total)


def fused(gallery, bank, test, gsize, qsize):
    cols, width = gallery.shape
    rb, rt = bank.shape[0], test.shape[0]
    cb = math.gcd(rb, 128)
    ct = math.gcd(rt, 64)
    chips, nb, nt = gsize // 2, rb // cb, rt // ct
    rows = gsize * rt
    tall = -(-rows // 128 // 8) * 8
    dma = lambda *shape: pltpu.SemaphoreType.DMA(shape)
    f32 = jnp.float32
    scores, norm, row = pl.pallas_call(
        functools.partial(kernel, gsize, qsize),
        out_shape=(
            jax.ShapeDtypeStruct((chips, 2, nt, ct, cols), f32),
            jax.ShapeDtypeStruct((cols // 128, 128), f32),
            jax.ShapeDtypeStruct((tall, 128), f32),
        ),
        in_specs=[pl.BlockSpec(memory_space=pltpu.HBM)] * 3,
        out_specs=(
            pl.BlockSpec(memory_space=pltpu.VMEM),
            pl.BlockSpec(memory_space=pltpu.VMEM),
            pl.BlockSpec(memory_space=pltpu.VMEM),
        ),
        scratch_shapes=[
            pltpu.VMEM((cols, width), jnp.bfloat16),
            pltpu.VMEM((chips, nb, 2, cb, width), jnp.bfloat16),
            pltpu.VMEM((chips, nt, 2, ct, width), jnp.bfloat16),
            pltpu.VMEM((8, cols), f32),
            pltpu.VMEM((8, cols), f32),
            pltpu.VMEM((rows, 128), f32),
            pltpu.VMEM((qsize, cols // 128, 128), f32),
            pltpu.VMEM((gsize, tall, 128), f32),
            dma(nb + nt + 1),
            dma(nb, chips), dma(nb, chips), dma(nb, chips), dma(nb, chips),
            dma(nt, chips), dma(nt, chips), dma(nt, chips), dma(nt, chips),
            dma(qsize), dma(qsize), dma(gsize), dma(gsize),
        ],
        compiler_params=pltpu.CompilerParams(
            collective_id=0, has_side_effects=True, vmem_limit_bytes=40 * 1024 * 1024
        ),
        cost_estimate=pl.CostEstimate(
            flops=2 * cols * width * gsize * (rb + rt),
            bytes_accessed=2 * width * (cols + rb + rt) + 4 * rows * cols,
            transcendentals=cols * gsize * (rb + rt),
        ),
    )(*(pltpu.with_memory_space_constraint(x, pltpu.HBM) for x in (gallery, bank, test)))
    return scores.reshape(rows, cols), norm.reshape(cols), row.reshape(-1)[:rows]


def per_device(gallery, querybank, test_queries):
    gsize, qsize = lax.axis_size("gal"), lax.axis_size("qb")
    bank_count = querybank.shape[1] * gsize * qsize
    offset = 2.0 * sharpness - math.log(bank_count)
    scores, normalizer, row_log = fused(gallery, querybank[0], test_queries[0], gsize, qsize)
    logprob = scores - (normalizer + offset)[None, :] - row_log[:, None]
    return (logprob, normalizer)


def solution(mesh):
    placed = (
        P(("slab", "gal"), None),
        P(("slab", "qb"), "gal", None),
        P(("slab", "qb"), "gal", None),
    )
    return jax.shard_map(
        per_device,
        mesh=mesh,
        in_specs=placed,
        out_specs=(P(("slab", "qb"), "gal"), P(("slab", "gal"))),
        check_vma=False,
    )
```

```python
import functools
import math

import jax
import jax.numpy as jnp
from jax import lax
from jax.experimental import pallas as pl
from jax.experimental.pallas import tpu as pltpu
from jax.sharding import PartitionSpec as P

sharpness = 20.0
LOG2E = math.log2(math.e)
MESH = pl.DeviceIdType.MESH
WINDOW = 3


def unit(values):
    wide = values.astype(jnp.float32)
    total = jnp.sum(wide * wide, axis=-1, keepdims=True)
    return (wide * lax.rsqrt(total + 1e-06)).astype(jnp.bfloat16)


def score(rows, gallery):
    return lax.dot_general(
        rows, gallery, (((1,), (1,)), ((), ())), preferred_element_type=jnp.float32
    )


def kernel(
    gsize, qsize, gallery_hbm, bank_hbm, test_hbm,
    s_buf, norm_out, row_out,
    gal, bank, test, acc, weight, lanes, zbuf, rbuf,
    load_sem, by_send, by_recv, bs_send, bs_recv,
    ty_send, ty_recv, ts_send, ts_recv, z_send, z_recv, r_send, r_recv,
):
    g = lax.axis_index("gal")
    q = lax.axis_index("qb")
    chips = gsize // 2
    y, core = g // 2, lax.rem(g, 2)
    sib = 2 * y + (1 - core)
    _, nb, _, cb, width = bank.shape
    _, nt, _, ct, _ = test.shape
    cols = gal.shape[0]
    bank_count = nb * cb * gsize * qsize

    loads = []
    for k in range(nb):
        loads.append(pltpu.make_async_copy(
            bank_hbm.at[pl.ds(k * cb, cb)], bank.at[y, k, core], load_sem.at[k]))
    for k in range(nt):
        loads.append(pltpu.make_async_copy(
            test_hbm.at[pl.ds(k * ct, ct)], test.at[y, k, core], load_sem.at[nb + k]))
    loads.append(pltpu.make_async_copy(gallery_hbm, gal, load_sem.at[nb + nt]))
    for copy in loads:
        copy.start()

    barrier = pltpu.get_barrier_semaphore()
    for d in range(1, gsize):
        pl.semaphore_signal(barrier, inc=1, device_id={"gal": lax.rem(g + d, gsize)}, device_id_type=MESH)
    for d in range(1, qsize):
        pl.semaphore_signal(barrier, inc=1, device_id={"qb": lax.rem(q + d, qsize)}, device_id_type=MESH)

    def across(array, sends, recvs, k, d):
        slot = array.at[y, k, core]
        there = lax.rem(y + d, chips)
        return pltpu.make_async_remote_copy(
            src_ref=slot, dst_ref=slot, send_sem=sends.at[k, d], recv_sem=recvs.at[k, d],
            device_id={"gal": 2 * there + core}, device_id_type=MESH)

    def arrival(array, sends, recvs, k, d):
        slot = array.at[lax.rem(y + chips - d, chips), k, core]
        return pltpu.make_async_remote_copy(
            src_ref=slot, dst_ref=slot, send_sem=sends.at[k, d], recv_sem=recvs.at[k, d],
            device_id={"gal": sib}, device_id_type=MESH)

    def beside(array, sends, recvs, k, d):
        slot = array.at[lax.rem(y + chips - d, chips), k, core]
        return pltpu.make_async_remote_copy(
            src_ref=slot, dst_ref=slot, send_sem=sends.at[k, d], recv_sem=recvs.at[k, d],
            device_id={"gal": sib}, device_id_type=MESH)

    def from_sib(array, sends, recvs, k, d):
        slot = array.at[lax.rem(y + chips - d, chips), k, 1 - core]
        return pltpu.make_async_remote_copy(
            src_ref=slot, dst_ref=slot, send_sem=sends.at[k, d], recv_sem=recvs.at[k, d],
            device_id={"gal": sib}, device_id_type=MESH)

    B = (bank, by_send, by_recv)
    BS = (bank, bs_send, bs_recv)
    T = (test, ty_send, ty_recv)
    TS = (test, ts_send, ts_recv)
    queue = [(B, BS, k) for k in range(nb)] + [(T, TS, k) for k in range(nt)]

    def push(i):
        if i < len(queue):
            far, near, k = queue[i]
            for d in range(1, chips):
                across(*far, k, d).start()

    for i, (far, near, k) in enumerate(queue):
        loads[i].wait()
        array = far[0]
        array[y, k, core] = unit(array[y, k, core])
        if i == 0:
            pl.semaphore_wait(barrier, gsize - 1 + qsize - 1)
        if i < WINDOW:
            push(i)
        beside(*near, k, 0).start()

    acc[...] = jnp.zeros_like(acc)
    loads[-1].wait()
    step_rows = math.gcd(cols, 64)

    @pl.loop(0, cols // step_rows)
    def _(i):
        at = pl.ds(pl.multiple_of(i * step_rows, step_rows), step_rows)
        gal[at, :] = unit(gal[at, :])

    block = math.gcd(cols, 512)

    def add_bank(slot, k):
        rows = bank[slot, k].reshape(2 * cb, width)
        for j in range(cols // block):
            at = slice(j * block, (j + 1) * block)
            part = score(rows, gal[at, :])
            part = jnp.exp2(part * (sharpness * LOG2E) - sharpness * LOG2E)
            acc[:, at] += jnp.sum(part.reshape(2 * cb // 8, 8, block), axis=0)

    def put_scores(slot, k):
        rows = test[slot, k].reshape(2 * ct, width)
        for j in range(cols // block):
            at = slice(j * block, (j + 1) * block)
            part = score(rows, gal[at, :]) * sharpness
            s_buf[slot, 0, k, :, at] = part[:ct]
            s_buf[slot, 1, k, :, at] = part[ct:]

    def row_pass(slot, k):
        for c in range(2):
            total = jnp.zeros((ct, 128), jnp.float32)
            for j in range(cols // 128):
                at = slice(j * 128, (j + 1) * 128)
                part = s_buf[slot, c, k, :, at]
                total += jnp.exp2(part * LOG2E - sharpness * LOG2E) * weight[0:1, at]
            at = pl.multiple_of(((slot * 2 + c) * nt + k) * ct, ct)
            lanes[pl.ds(at, ct), :] = total

    for k in range(nb):
        from_sib(*BS, k, 0).wait_recv()
        add_bank(y, k)
    for k in range(nt):
        from_sib(*TS, k, 0).wait_recv()
        put_scores(y, k)

    pending = None
    for i, (far, near, k) in enumerate(queue[:nb]):
        for d in range(1, chips):
            arrival(*far, k, d).wait_recv()
            beside(*near, k, d).start()
            across(*far, k, d).wait_send()
        push(i + WINDOW)
        if pending is not None:
            for d in range(1, chips):
                from_sib(*BS, pending, d).wait_recv()
                add_bank(lax.rem(y + chips - d, chips), pending)
        pending = k
    for d in range(1, chips):
        from_sib(*BS, pending, d).wait_recv()
        add_bank(lax.rem(y + chips - d, chips), pending)

    column = jnp.sum(acc[...], axis=0, keepdims=True)
    for j in range(cols // 128):
        zbuf[0, j:j + 1, :] = column[:, j * 128:(j + 1) * 128]

    def z_copy(d):
        return pltpu.make_async_remote_copy(
            src_ref=zbuf.at[0], dst_ref=zbuf.at[d], send_sem=z_send.at[d], recv_sem=z_recv.at[d],
            device_id={"qb": lax.rem(q + d, qsize)}, device_id_type=MESH)

    for d in range(1, qsize):
        z_copy(d).start()
    pending = None
    for i, (far, near, k) in enumerate(queue[nb:]):
        for d in range(1, chips):
            arrival(*far, k, d).wait_recv()
            beside(*near, k, d).start()
            across(*far, k, d).wait_send()
        push(nb + i + WINDOW)
        if pending is not None:
            for d in range(1, chips):
                slot = lax.rem(y + chips - d, chips)
                from_sib(*TS, pending, d).wait_recv()
                put_scores(slot, pending)
        pending = k
    for d in range(1, chips):
        slot = lax.rem(y + chips - d, chips)
        from_sib(*TS, pending, d).wait_recv()
        put_scores(slot, pending)

    for d in range(1, qsize):
        z_copy(d).wait_recv()
    total = zbuf[0]
    for d in range(1, qsize):
        total += zbuf[d]
    norm_out[...] = sharpness + jnp.log(total)
    scale = (bank_count * math.exp(-2.0 * sharpness)) / total
    for j in range(cols // 128):
        weight[0:1, j * 128:(j + 1) * 128] = scale[j:j + 1, :]
    for slot in range(chips):
        for k in range(nt):
            row_pass(slot, k)

    rows = lanes.shape[0]
    rbuf[0] = jnp.zeros_like(rbuf[0])
    sums = jnp.sum(lanes[...].T, axis=0, keepdims=True)
    for j in range(rows // 128):
        rbuf[0, j:j + 1, :] = sums[:, j * 128:(j + 1) * 128]

    def r_copy(d):
        return pltpu.make_async_remote_copy(
            src_ref=rbuf.at[0], dst_ref=rbuf.at[d], send_sem=r_send.at[d], recv_sem=r_recv.at[d],
            device_id={"gal": lax.rem(g + d, gsize)}, device_id_type=MESH)

    for d in range(1, gsize):
        r_copy(d).start()
    for i, (far, near, k) in enumerate(queue):
        for d in range(chips):
            beside(*near, k, d).wait_send()
    for d in range(1, qsize):
        z_copy(d).wait_send()
    for d in range(1, gsize):
        r_copy(d).wait()
    total = rbuf[0]
    for d in range(1, gsize):
        total += rbuf[d]
    row_out[...] = jnp.log(total)


def fused(gallery, bank, test, gsize, qsize):
    cols, width = gallery.shape
    rb, rt = bank.shape[0], test.shape[0]
    cb = math.gcd(rb, 128)
    ct = math.gcd(rt, 64)
    chips, nb, nt = gsize // 2, rb // cb, rt // ct
    rows = gsize * rt
    tall = -(-rows // 128 // 8) * 8
    dma = lambda *shape: pltpu.SemaphoreType.DMA(shape)
    f32 = jnp.float32
    scores, norm, row = pl.pallas_call(
        functools.partial(kernel, gsize, qsize),
        out_shape=(
            jax.ShapeDtypeStruct((chips, 2, nt, ct, cols), f32),
            jax.ShapeDtypeStruct((cols // 128, 128), f32),
            jax.ShapeDtypeStruct((tall, 128), f32),
        ),
        in_specs=[pl.BlockSpec(memory_space=pltpu.HBM)] * 3,
        out_specs=(
            pl.BlockSpec(memory_space=pltpu.VMEM),
            pl.BlockSpec(memory_space=pltpu.VMEM),
            pl.BlockSpec(memory_space=pltpu.VMEM),
        ),
        scratch_shapes=[
            pltpu.VMEM((cols, width), jnp.bfloat16),
            pltpu.VMEM((chips, nb, 2, cb, width), jnp.bfloat16),
            pltpu.VMEM((chips, nt, 2, ct, width), jnp.bfloat16),
            pltpu.VMEM((8, cols), f32),
            pltpu.VMEM((8, cols), f32),
            pltpu.VMEM((rows, 128), f32),
            pltpu.VMEM((qsize, cols // 128, 128), f32),
            pltpu.VMEM((gsize, tall, 128), f32),
            dma(nb + nt + 1),
            dma(nb, chips), dma(nb, chips), dma(nb, chips), dma(nb, chips),
            dma(nt, chips), dma(nt, chips), dma(nt, chips), dma(nt, chips),
            dma(qsize), dma(qsize), dma(gsize), dma(gsize),
        ],
        compiler_params=pltpu.CompilerParams(
            collective_id=0, has_side_effects=True, vmem_limit_bytes=40 * 1024 * 1024
        ),
        cost_estimate=pl.CostEstimate(
            flops=2 * cols * width * gsize * (rb + rt),
            bytes_accessed=2 * width * (cols + rb + rt) + 4 * rows * cols,
            transcendentals=cols * gsize * (rb + rt),
        ),
    )(*(pltpu.with_memory_space_constraint(x, pltpu.HBM) for x in (gallery, bank, test)))
    return scores.reshape(rows, cols), norm.reshape(cols), row.reshape(-1)[:rows]


def per_device(gallery, querybank, test_queries):
    gsize, qsize = lax.axis_size("gal"), lax.axis_size("qb")
    bank_count = querybank.shape[1] * gsize * qsize
    offset = 2.0 * sharpness - math.log(bank_count)
    scores, normalizer, row_log = fused(gallery, querybank[0], test_queries[0], gsize, qsize)
    logprob = scores - (normalizer + offset)[None, :] - row_log[:, None]
    return (logprob, normalizer)


def solution(mesh):
    placed = (
        P(("slab", "gal"), None),
        P(("slab", "qb"), "gal", None),
        P(("slab", "qb"), "gal", None),
    )
    return jax.shard_map(
        per_device,
        mesh=mesh,
        in_specs=placed,
        out_specs=(P(("slab", "qb"), "gal"), P(("slab", "gal"))),
        check_vma=False,
    )
```

```python
import functools
import math

import jax
import jax.numpy as jnp
from jax import lax
from jax.experimental import pallas as pl
from jax.experimental.pallas import tpu as pltpu
from jax.sharding import PartitionSpec as P

sharpness = 20.0
LOG2E = math.log2(math.e)
MESH = pl.DeviceIdType.MESH
WINDOW = 3


def unit(values):
    wide = values.astype(jnp.float32)
    total = jnp.sum(wide * wide, axis=-1, keepdims=True)
    return (wide * lax.rsqrt(total + 1e-06)).astype(jnp.bfloat16)


def score(rows, gallery):
    return lax.dot_general(
        rows, gallery, (((1,), (1,)), ((), ())), preferred_element_type=jnp.float32
    )


def kernel(
    gsize, qsize, gallery_hbm, bank_hbm, test_hbm,
    s_buf, norm_out, row_out,
    gal, bank, test, acc, weight, lanes, zbuf, rbuf,
    load_sem, by_send, by_recv, bs_send, bs_recv,
    ty_send, ty_recv, ts_send, ts_recv, z_send, z_recv, r_send, r_recv,
):
    g = lax.axis_index("gal")
    q = lax.axis_index("qb")
    chips = gsize // 2
    y, core = g // 2, lax.rem(g, 2)
    sib = 2 * y + (1 - core)
    _, nb, _, cb, width = bank.shape
    _, nt, _, ct, _ = test.shape
    cols = gal.shape[0]
    bank_count = nb * cb * gsize * qsize

    loads = []
    for k in range(nb):
        loads.append(pltpu.make_async_copy(
            bank_hbm.at[pl.ds(k * cb, cb)], bank.at[y, k, core], load_sem.at[k]))
    for k in range(nt):
        loads.append(pltpu.make_async_copy(
            test_hbm.at[pl.ds(k * ct, ct)], test.at[y, k, core], load_sem.at[nb + k]))
    loads.append(pltpu.make_async_copy(gallery_hbm, gal, load_sem.at[nb + nt]))
    for copy in loads:
        copy.start()

    barrier = pltpu.get_barrier_semaphore()
    for d in range(1, gsize):
        pl.semaphore_signal(barrier, inc=1, device_id={"gal": lax.rem(g + d, gsize)}, device_id_type=MESH)
    for d in range(1, qsize):
        pl.semaphore_signal(barrier, inc=1, device_id={"qb": lax.rem(q + d, qsize)}, device_id_type=MESH)

    def across(array, sends, recvs, k, d):
        slot = array.at[y, k, core]
        there = lax.rem(y + d, chips)
        return pltpu.make_async_remote_copy(
            src_ref=slot, dst_ref=slot, send_sem=sends.at[k, d], recv_sem=recvs.at[k, d],
            device_id={"gal": 2 * there + core}, device_id_type=MESH)

    def arrival(array, sends, recvs, k, d):
        slot = array.at[lax.rem(y + chips - d, chips), k, core]
        return pltpu.make_async_remote_copy(
            src_ref=slot, dst_ref=slot, send_sem=sends.at[k, d], recv_sem=recvs.at[k, d],
            device_id={"gal": sib}, device_id_type=MESH)

    def beside(array, sends, recvs, k, d):
        slot = array.at[lax.rem(y + chips - d, chips), k, core]
        return pltpu.make_async_remote_copy(
            src_ref=slot, dst_ref=slot, send_sem=sends.at[k, d], recv_sem=recvs.at[k, d],
            device_id={"gal": sib}, device_id_type=MESH)

    def from_sib(array, sends, recvs, k, d):
        slot = array.at[lax.rem(y + chips - d, chips), k, 1 - core]
        return pltpu.make_async_remote_copy(
            src_ref=slot, dst_ref=slot, send_sem=sends.at[k, d], recv_sem=recvs.at[k, d],
            device_id={"gal": sib}, device_id_type=MESH)

    B = (bank, by_send, by_recv)
    BS = (bank, bs_send, bs_recv)
    T = (test, ty_send, ty_recv)
    TS = (test, ts_send, ts_recv)
    queue = [(B, BS, k) for k in range(nb)] + [(T, TS, k) for k in range(nt)]

    def push(i):
        if i < len(queue):
            far, near, k = queue[i]
            for d in range(1, chips):
                across(*far, k, d).start()

    for i, (far, near, k) in enumerate(queue):
        loads[i].wait()
        array = far[0]
        array[y, k, core] = unit(array[y, k, core])
        if i == 0:
            pl.semaphore_wait(barrier, gsize - 1 + qsize - 1)
        if i < WINDOW:
            push(i)
        beside(*near, k, 0).start()

    acc[...] = jnp.zeros_like(acc)
    loads[-1].wait()
    step_rows = math.gcd(cols, 64)

    @pl.loop(0, cols // step_rows)
    def _(i):
        at = pl.ds(pl.multiple_of(i * step_rows, step_rows), step_rows)
        gal[at, :] = unit(gal[at, :])

    block = math.gcd(cols, 512)

    def add_bank(slot, k):
        rows = bank[slot, k].reshape(2 * cb, width)
        for j in range(cols // block):
            at = slice(j * block, (j + 1) * block)
            part = score(rows, gal[at, :])
            part = jnp.exp2(part * (sharpness * LOG2E) - sharpness * LOG2E)
            acc[:, at] += jnp.sum(part.reshape(2 * cb // 8, 8, block), axis=0)

    def put_scores(slot, k):
        rows = test[slot, k].reshape(2 * ct, width)
        for j in range(cols // block):
            at = slice(j * block, (j + 1) * block)
            part = score(rows, gal[at, :]) * sharpness
            s_buf[slot, 0, k, :, at] = part[:ct]
            s_buf[slot, 1, k, :, at] = part[ct:]

    def row_pass(slot, k):
        for c in range(2):
            total = jnp.zeros((ct, 128), jnp.float32)
            for j in range(cols // 128):
                at = slice(j * 128, (j + 1) * 128)
                part = s_buf[slot, c, k, :, at]
                total += jnp.exp2(part * LOG2E - sharpness * LOG2E) * weight[0:1, at]
            at = pl.multiple_of(((slot * 2 + c) * nt + k) * ct, ct)
            lanes[pl.ds(at, ct), :] = total

    for k in range(nb):
        from_sib(*BS, k, 0).wait_recv()
        add_bank(y, k)
    for k in range(nt):
        from_sib(*TS, k, 0).wait_recv()
        put_scores(y, k)

    pending = None
    for i, (far, near, k) in enumerate(queue[:nb]):
        for d in range(1, chips):
            arrival(*far, k, d).wait_recv()
            beside(*near, k, d).start()
            across(*far, k, d).wait_send()
        push(i + WINDOW)
        if pending is not None:
            for d in range(1, chips):
                from_sib(*BS, pending, d).wait_recv()
                add_bank(lax.rem(y + chips - d, chips), pending)
        pending = k
    for d in range(1, chips):
        from_sib(*BS, pending, d).wait_recv()
        add_bank(lax.rem(y + chips - d, chips), pending)

    column = jnp.sum(acc[...], axis=0, keepdims=True)
    for j in range(cols // 128):
        zbuf[0, j:j + 1, :] = column[:, j * 128:(j + 1) * 128]

    def z_copy(d):
        return pltpu.make_async_remote_copy(
            src_ref=zbuf.at[0], dst_ref=zbuf.at[d], send_sem=z_send.at[d], recv_sem=z_recv.at[d],
            device_id={"qb": lax.rem(q + d, qsize)}, device_id_type=MESH)

    for d in range(1, qsize):
        z_copy(d).start()
    pending = None
    for i, (far, near, k) in enumerate(queue[nb:]):
        for d in range(1, chips):
            arrival(*far, k, d).wait_recv()
            beside(*near, k, d).start()
            across(*far, k, d).wait_send()
        push(nb + i + WINDOW)
        if pending is not None:
            for d in range(1, chips):
                slot = lax.rem(y + chips - d, chips)
                from_sib(*TS, pending, d).wait_recv()
                put_scores(slot, pending)
        pending = k
    for d in range(1, chips):
        slot = lax.rem(y + chips - d, chips)
        from_sib(*TS, pending, d).wait_recv()
        put_scores(slot, pending)

    for d in range(1, qsize):
        z_copy(d).wait_recv()
    total = zbuf[0]
    for d in range(1, qsize):
        total += zbuf[d]
    norm_out[...] = sharpness + jnp.log(total)
    scale = (bank_count * math.exp(-2.0 * sharpness)) / total
    for j in range(cols // 128):
        weight[0:1, j * 128:(j + 1) * 128] = scale[j:j + 1, :]
    for slot in range(chips):
        for k in range(nt):
            row_pass(slot, k)

    rows = lanes.shape[0]
    rbuf[0] = jnp.zeros_like(rbuf[0])
    sums = jnp.sum(lanes[...].T, axis=0, keepdims=True)
    for j in range(rows // 128):
        rbuf[0, j:j + 1, :] = sums[:, j * 128:(j + 1) * 128]

    def r_copy(d):
        return pltpu.make_async_remote_copy(
            src_ref=rbuf.at[0], dst_ref=rbuf.at[d], send_sem=r_send.at[d], recv_sem=r_recv.at[d],
            device_id={"gal": lax.rem(g + d, gsize)}, device_id_type=MESH)

    for d in range(1, gsize):
        r_copy(d).start()
    for i, (far, near, k) in enumerate(queue):
        for d in range(chips):
            beside(*near, k, d).wait_send()
    for d in range(1, qsize):
        z_copy(d).wait_send()
    for d in range(1, gsize):
        r_copy(d).wait()
    total = rbuf[0]
    for d in range(1, gsize):
        total += rbuf[d]
    row_out[...] = jnp.log(total)


def fused(gallery, bank, test, gsize, qsize):
    cols, width = gallery.shape
    rb, rt = bank.shape[0], test.shape[0]
    cb = math.gcd(rb, 128)
    ct = math.gcd(rt, 64)
    chips, nb, nt = gsize // 2, rb // cb, rt // ct
    rows = gsize * rt
    tall = -(-rows // 128 // 8) * 8
    dma = lambda *shape: pltpu.SemaphoreType.DMA(shape)
    f32 = jnp.float32
    scores, norm, row = pl.pallas_call(
        functools.partial(kernel, gsize, qsize),
        out_shape=(
            jax.ShapeDtypeStruct((chips, 2, nt, ct, cols), f32),
            jax.ShapeDtypeStruct((cols // 128, 128), f32),
            jax.ShapeDtypeStruct((tall, 128), f32),
        ),
        in_specs=[pl.BlockSpec(memory_space=pltpu.HBM)] * 3,
        out_specs=(
            pl.BlockSpec(memory_space=pltpu.VMEM),
            pl.BlockSpec(memory_space=pltpu.VMEM),
            pl.BlockSpec(memory_space=pltpu.VMEM),
        ),
        scratch_shapes=[
            pltpu.VMEM((cols, width), jnp.bfloat16),
            pltpu.VMEM((chips, nb, 2, cb, width), jnp.bfloat16),
            pltpu.VMEM((chips, nt, 2, ct, width), jnp.bfloat16),
            pltpu.VMEM((8, cols), f32),
            pltpu.VMEM((8, cols), f32),
            pltpu.VMEM((rows, 128), f32),
            pltpu.VMEM((qsize, cols // 128, 128), f32),
            pltpu.VMEM((gsize, tall, 128), f32),
            dma(nb + nt + 1),
            dma(nb, chips), dma(nb, chips), dma(nb, chips), dma(nb, chips),
            dma(nt, chips), dma(nt, chips), dma(nt, chips), dma(nt, chips),
            dma(qsize), dma(qsize), dma(gsize), dma(gsize),
        ],
        compiler_params=pltpu.CompilerParams(
            collective_id=0, has_side_effects=True, vmem_limit_bytes=40 * 1024 * 1024
        ),
        cost_estimate=pl.CostEstimate(
            flops=2 * cols * width * gsize * (rb + rt),
            bytes_accessed=2 * width * (cols + rb + rt) + 4 * rows * cols,
            transcendentals=cols * gsize * (rb + rt),
        ),
    )(*(pltpu.with_memory_space_constraint(x, pltpu.HBM) for x in (gallery, bank, test)))
    return scores.reshape(rows, cols), norm, row


def finish(offset, s_ref, norm_ref, row_ref, out_hbm, norm_hbm, buf, sem, norm_sem):
    rows, cols = s_ref.shape
    norm_copy = pltpu.make_async_copy(norm_ref, norm_hbm, norm_sem)
    norm_copy.start()
    copies = []
    for i in range(rows // 128):
        at = slice(i * 128, (i + 1) * 128)
        own = jnp.broadcast_to(row_ref[i:i + 1, :], (128, 128)).T + offset
        for j in range(cols // 128):
            to = slice(j * 128, (j + 1) * 128)
            buf[at, to] = s_ref[at, to] - norm_ref[j:j + 1, :] - own
        for h in range(2):
            part = pl.ds(i * 128 + h * 64, 64)
            copy = pltpu.make_async_copy(buf.at[part], out_hbm.at[part], sem.at[2 * i + h])
            copy.start()
            copies.append(copy)
    for copy in copies:
        copy.wait()
    norm_copy.wait()


def per_device(gallery, querybank, test_queries):
    gsize, qsize = lax.axis_size("gal"), lax.axis_size("qb")
    bank_count = querybank.shape[1] * gsize * qsize
    offset = 2.0 * sharpness - math.log(bank_count)
    scores, normalizer, row_log = fused(gallery, querybank[0], test_queries[0], gsize, qsize)
    rows, cols = scores.shape
    logprob, normalizer = pl.pallas_call(
        functools.partial(finish, offset),
        out_shape=(
            jax.ShapeDtypeStruct((rows, cols), jnp.float32),
            jax.ShapeDtypeStruct(normalizer.shape, jnp.float32),
        ),
        in_specs=[pl.BlockSpec(memory_space=pltpu.VMEM)] * 3,
        out_specs=[pl.BlockSpec(memory_space=pltpu.HBM)] * 2,
        scratch_shapes=[
            pltpu.VMEM((rows, cols), jnp.float32),
            pltpu.SemaphoreType.DMA((rows // 64,)),
            pltpu.SemaphoreType.DMA(()),
        ],
        compiler_params=pltpu.CompilerParams(vmem_limit_bytes=16 * 1024 * 1024),
    )(scores, normalizer, row_log)
    normalizer = normalizer.reshape(-1)
    return (logprob, normalizer)


def solution(mesh):
    placed = (
        P(("slab", "gal"), None),
        P(("slab", "qb"), "gal", None),
        P(("slab", "qb"), "gal", None),
    )
    return jax.shard_map(
        per_device,
        mesh=mesh,
        in_specs=placed,
        out_specs=(P(("slab", "qb"), "gal"), P(("slab", "gal"))),
        check_vma=False,
    )
```
